256 devices in a mesh: dp: 8 (over z), mp: 32 (over y, x, core).
Axes of the slice: x: 4, y: 4, z: 8, core: 2. Of those that a mesh axis runs over, the one named last changes fastest.
Arguments:
- hidden_acts: bfloat16 [5120, 28672], P('dp', 'mp'), may hold values from -6 to 6
- out_grads: bfloat16 [5120, 8192], P('dp', 'mp'), may hold values from -6 to 6
- query_in: bfloat16 [64, 32, 28672], P('dp', None, 'mp'), may hold values from -0.0625 to 0.0625
- query_out: bfloat16 [64, 32, 8192], P('dp', None, 'mp'), may hold values from -0.125 to 0.125
- seq_ids: int32 [8, 640], P('dp'), may hold values from 0 to 15, never falling along the last dimension, each value on 1 to 80 neighbouring positions
Outputs:
- scores: float32 [128, 64], P('dp', 'mp')
The draws below stay inside these ranges and needn't reach their ends.
Inputs may be any that keep to these rules, and one draw needn't show every extreme that they name: `seq_ids`: in each row, ids never fall along the tokens, and every id of 0 to 15 covers 1 to 80 tokens, one exactly 80.
All inputs are finite; a program needn't handle non-finite values.
Results may differ from the reference program's by a relative error of at most 0.0003.
Values may be sent and summed in bfloat16 or wider, within the bound.
A program may use at most 64 MiB of HBM per device.

```python
import math
import jax
import jax.numpy as jnp
import numpy as np
from jax import lax

D = 8192
FF = 28672
Q = 64
R = 32
TOK_G = 640
SEQS = 16
MOST = 80
GROUPS = 8
TOKENS = 5120
N_DP = 8


def strengthened(result, rng, source, target, parts, factor):
    def block_of(position):
        return (jnp.arange(result.shape[position]) // (result.shape[position] // parts)).reshape((-1,) + (1,) * (result.ndim - 1 - position))

    one_side = jax.random.permutation(rng, parts)[block_of(target)]
    far = (block_of(target) + parts // 2) % parts
    return jnp.where((block_of(source) == one_side) | (block_of(source) == far), factor * result, result)


def block_scale(key, extent, split, least, top_value):
    loudness, own = 1.0, jax.random.fold_in(key, 6)
    for axis_at, blocks in split:
        steps = jnp.exp(jax.random.uniform(jax.random.fold_in(own, axis_at), (blocks,), jnp.float32, least / len(split), top_value / len(split)))
        loudness = loudness * jnp.repeat(steps, extent[axis_at] // blocks).reshape([-1 if axis == axis_at else 1 for axis in range(len(extent))])
    return loudness


def profile(number_of, total, bound, lean):
    loads = [(1 << 20) // math.isqrt(grade ** lean) + 1 for grade in range(2, number_of + 1)]
    spare, holding = total - bound - (number_of - 1), [1] * (number_of - 1)
    while spare > 0:
        movable = [i for i in range(number_of - 1) if holding[i] < bound]
        pool, left = sum([loads[i] for i in movable]), spare
        for i in movable:
            more = min(bound - holding[i], max(1, left * loads[i] // pool), spare)
            holding[i] = holding[i] + more
            spare = spare - more
    return np.array([bound] + holding)


def ragged_sizes(key, number_of, total, most, skew):
    if number_of == 2:
        one = jax.random.randint(key, (), max(1, total - most), min(most, total - 1) + 1)
        return jnp.stack([one, total - one])
    lengths = jnp.asarray(profile(number_of, total, most, skew), jnp.int32)
    couples = (number_of - 1) // 2
    donor, receiver = lengths[1:1 + 2 * couples:2], lengths[2:2 + 2 * couples:2]
    slack = jnp.minimum(donor - 1, most - receiver)
    shifted = jax.random.randint(jax.random.fold_in(key, 1), (couples,), 0, 1 << 20) % (slack + 1)
    lengths = lengths.at[1:1 + 2 * couples:2].set(donor - shifted).at[2:2 + 2 * couples:2].set(receiver + shifted)
    return lengths[jax.random.permutation(jax.random.fold_in(key, 2), number_of)]


def normal_values(key, dims, width, reach, split=(), kind=jnp.bfloat16):
    level = block_scale(key, dims, split, -0.22, 0.18) if split else 1.0
    result = jax.random.normal(key, dims, jnp.float32) * width * level
    return jnp.minimum(jnp.maximum(result, -reach), reach).astype(kind)


def bell_draw_with(stream_key, extent, spread, bound, shards, heavy, kind=jnp.bfloat16):
    values = spread * jax.random.normal(stream_key, extent, jnp.float32)
    if shards:
        values = values * block_scale(stream_key, extent, shards, -0.22, 0.18)
    return jnp.clip(strengthened(values, jax.random.fold_in(stream_key, 3), *heavy), -bound, bound).astype(kind)


def setup_inputs(seed: int = 0) -> dict:
    splits = jax.random.split(jax.random.key(seed), 6)
    return {
        "hidden_acts": normal_values(splits[0], (TOKENS, FF), 1.0, 6.0, ((0, 8), (1, 32))),
        "out_grads": normal_values(splits[1], (TOKENS, D), 1.0, 6.0, ((0, 8), (1, 32))),
        "query_in": bell_draw_with(splits[2], (Q, R, FF), FF ** -0.5, 0.0625, ((0, 8), (2, 32)), (2, 0, 32, 2.75)),
        "query_out": bell_draw_with(splits[3], (Q, R, D), D ** -0.5, 0.125, ((0, 8), (2, 32)), (2, 0, 32, 2.75)),
        "seq_ids": jax.vmap(lambda own: jnp.searchsorted(jnp.cumsum(ragged_sizes(own, SEQS, TOK_G, MOST, 1)), jnp.arange(TOK_G), side="right"))(jax.random.split(splits[4], GROUPS)).reshape((GROUPS, TOK_G)).astype(jnp.int32),
    }


def reference(hidden_acts, out_grads, query_in, query_out, seq_ids):
    in_rows = query_in.reshape(Q * R, FF)
    out_rows = query_out.reshape(Q * R, D)
    in_proj = lax.dot_general(hidden_acts, in_rows, (((1,), (1,)), ((), ())), preferred_element_type=jnp.float32)
    out_proj = lax.dot_general(out_grads, out_rows, (((1,), (1,)), ((), ())), preferred_element_type=jnp.float32)
    token_score = (in_proj * out_proj).reshape(TOKENS, Q, R).sum(axis=2)
    token_score = token_score.reshape(N_DP, TOK_G, Q)
    labels = jnp.arange(SEQS, dtype=jnp.int32)
    onehot = (seq_ids[:, None, :] == labels[None, :, None]).astype(jnp.float32)
    summed = jnp.einsum('gst,gtq->gsq', onehot, token_score, precision=lax.Precision.HIGHEST)
    return summed.reshape(N_DP * SEQS, Q) / math.sqrt(R * TOK_G / SEQS)
```

```python
import functools
import math

import jax
import jax.numpy as jnp
from jax import lax
from jax.experimental import pallas as pl
from jax.experimental.pallas import tpu as pltpu
from jax.sharding import PartitionSpec as P

R = 32
TOK = 640
SEQS = 16
NZ = 8
SIDE = 4
CHIPS = SIDE * SIDE
QH = 4
MESH = pl.DeviceIdType.MESH
NT = (((1,), (1,)), ((), ()))
SCALE = 1.0 / math.sqrt(R * TOK / SEQS)


def kernel(
    hid, grad, q_in, q_out, seq, out,
    h_buf, g_buf, own_a, own_b, ring_a, ring_b, part, got, last, landed,
    loc_sem, sib_send, sib_recv, z_send, z_recv, a_send, a_recv, f_send, f_recv,
):
    z, m = lax.axis_index("dp"), lax.axis_index("mp")
    core = lax.rem(m, 2)
    chip = m // 2
    y, x = chip // SIDE, lax.rem(chip, SIDE)
    sibling = (z, chip * 2 + 1 - core)
    along = ((lax.rem(z + 1, NZ), m), (lax.rem(z + NZ - 1, NZ), m))

    mine = pl.ds(core * QH, QH)
    local = [
        pltpu.make_async_copy(src, dst, loc_sem.at[i])
        for i, (src, dst) in enumerate((
            (q_in.at[mine], own_a.at[0]),
            (q_out.at[mine], own_b.at[0]),
            (hid, h_buf.at[0]),
            (grad, g_buf.at[0]),
        ))
    ]
    for copy in local:
        copy.start()

    ready = pltpu.get_barrier_semaphore()
    for target in along:
        pl.semaphore_signal(ready, inc=1, device_id=target, device_id_type=MESH)

    def greet(k, carry):
        pl.semaphore_signal(ready, inc=1, device_id=(z, lax.rem(m + k, 2 * CHIPS)), device_id_type=MESH)
        return carry

    lax.fori_loop(1, 2 * CHIPS, greet, 0)
    pl.semaphore_wait(ready, 2 * CHIPS + 1)

    def to_sibling(i, src, dst):
        return pltpu.make_async_remote_copy(src, dst, sib_send.at[i], sib_recv.at[i], sibling, MESH)

    theirs = pl.ds((1 - core) * QH, QH)
    swap = [
        to_sibling(0, q_in.at[theirs], own_a.at[1]),
        to_sibling(1, q_out.at[theirs], own_b.at[1]),
        to_sibling(2, hid, h_buf.at[1]),
        to_sibling(3, grad, g_buf.at[1]),
    ]

    def hop(d, s, j):
        if s > 0:
            a, b = ring_a.at[d, s - 1, j], ring_b.at[d, s - 1, j]
        elif j == 0:
            a, b = q_in.at[mine], q_out.at[mine]
        else:
            a, b = own_a.at[1], own_b.at[1]
        return [
            pltpu.make_async_remote_copy(
                src, dst.at[d, s, j], z_send.at[d, s, j, i], z_recv.at[d, s, j, i], along[d], MESH
            )
            for i, (src, dst) in enumerate(((a, ring_a), (b, ring_b)))
        ]

    hops = {(d, s, j): hop(d, s, j) for s in range(4) for j in range(2) for d in range(2) if s < 3 or d == j}

    def start(copies):
        for copy in copies:
            copy.start()

    def arrived(copies):
        for copy in copies:
            copy.wait_recv()

    start(swap[:2])
    for d in range(2):
        start(hops[d, 0, 0])
    start(swap[2:])
    arrived(swap[:2])
    for d in range(2):
        start(hops[d, 0, 1])

    def project(p, halves):
        for at, blocks, tokens in ((0, 0, h_buf), (8, 1, g_buf)):
            total = None
            for j, half in enumerate(halves):
                rows = half[blocks][...].reshape(QH * R, tokens.shape[2])
                term = lax.dot_general(rows, tokens[j], NT, preferred_element_type=jnp.float32)
                total = term if total is None else total + term
            part[p, :, at : at + 8, :] = total.reshape(CHIPS, 8, TOK)

    def peer(k):
        return lax.rem(y + k // SIDE, SIDE) * SIDE + lax.rem(x + lax.rem(k, SIDE), SIDE)

    def spread(p):
        def send(k, carry):
            target = peer(k)
            pltpu.make_async_remote_copy(
                part.at[p, target], got.at[p, k - 1], a_send.at[p], a_recv.at[p], (z, target * 2 + core), MESH
            ).start()
            return carry

        lax.fori_loop(1, CHIPS, send, 0)

    label = lax.broadcasted_iota(jnp.int32, (SEQS, TOK), 0)
    member = seq[...] == label

    def add_up(p):
        pltpu.make_async_copy(got.at[p], got.at[p], a_recv.at[p]).wait()
        total = part[p, chip]
        for k in range(CHIPS - 1):
            total = total + got[p, k]
        score = jnp.sum(total[:8] * total[8:], axis=0, keepdims=True)
        by_seq = jnp.where(member, score, 0.0)
        lanes = by_seq[:, :128]
        for t in range(1, TOK // 128):
            lanes = lanes + by_seq[:, t * 128 : (t + 1) * 128]
        last[p] = lanes

    def final_copy(p, step):
        origin = lax.rem(z + step + NZ, NZ)
        owner = (2 * origin + core) * 2 + chip // 8
        slot = lax.rem(chip, 8)
        away = pltpu.make_async_remote_copy(
            last.at[p], landed.at[slot], f_send.at[p], f_recv.at[0], (z, owner), MESH
        )
        here = pltpu.make_async_copy(last.at[p], landed.at[slot], f_recv.at[0])
        return owner == m, away, here

    steps = [0, -1, 1, -2, 2, -3, 3, 4]

    def finish(p):
        add_up(p)
        own, away, here = final_copy(p, steps[p])
        pl.when(own)(here.start)
        pl.when(jnp.logical_not(own))(away.start)

    for copy in local:
        copy.wait()
    arrived(swap[2:])
    project(0, [(own_a.at[0], own_b.at[0]), (own_a.at[1], own_b.at[1])])
    spread(0)
    for s in range(3):
        for j in range(2):
            for d in range(2):
                arrived(hops[d, s, j])
                if (d, s + 1, j) in hops:
                    start(hops[d, s + 1, j])
        for d in range(2):
            p = 1 + 2 * s + d
            project(p, [(ring_a.at[d, s, j], ring_b.at[d, s, j]) for j in range(2)])
            spread(p)
        for p in ([0] if s == 0 else [2 * s - 1, 2 * s]):
            finish(p)
    for d in range(2):
        arrived(hops[d, 3, d])
    project(7, [(ring_a.at[j, 3, j], ring_b.at[j, 3, j]) for j in range(2)])
    spread(7)
    for p in (5, 6, 7):
        finish(p)

    for copy in swap:
        copy.wait_send()
    for copies in hops.values():
        for copy in copies:
            copy.wait_send()
    for p in range(NZ):
        pltpu.make_async_copy(got.at[p], got.at[p], a_send.at[p]).wait()
        own, away, here = final_copy(p, steps[p])
        pl.when(jnp.logical_not(own))(away.wait_send)

    pltpu.make_async_copy(landed, landed, f_recv.at[0]).wait()
    for q in range(2):
        total = (landed[4 * q] + landed[4 * q + 1]) + (landed[4 * q + 2] + landed[4 * q + 3])
        out[:, q : q + 1] = jnp.sum(total, axis=1, keepdims=True) * SCALE


def body(hidden_acts, out_grads, query_in, query_out, seq_ids):
    ff, width = hidden_acts.shape[1], out_grads.shape[1]
    any_spec = pl.BlockSpec(memory_space=pl.ANY)
    vmem_spec = pl.BlockSpec(memory_space=pltpu.VMEM)
    dma = pltpu.SemaphoreType.DMA
    bf16, f32 = jnp.bfloat16, jnp.float32
    return pl.pallas_call(
        kernel,
        out_shape=jax.ShapeDtypeStruct((SEQS, 2), f32),
        in_specs=[any_spec] * 4 + [vmem_spec],
        out_specs=vmem_spec,
        scratch_shapes=[
            pltpu.VMEM((2, TOK, ff), bf16),
            pltpu.VMEM((2, TOK, width), bf16),
            pltpu.VMEM((2, QH, R, ff), bf16),
            pltpu.VMEM((2, QH, R, width), bf16),
            pltpu.VMEM((2, 4, 2, QH, R, ff), bf16),
            pltpu.VMEM((2, 4, 2, QH, R, width), bf16),
            pltpu.VMEM((NZ, CHIPS, 16, TOK), f32),
            pltpu.VMEM((NZ, CHIPS - 1, 16, TOK), f32),
            pltpu.VMEM((NZ, SEQS, 128), f32),
            pltpu.VMEM((8, SEQS, 128), f32),
            dma((4,)),
            dma((4,)),
            dma((4,)),
            dma((2, 4, 2, 2)),
            dma((2, 4, 2, 2)),
            dma((NZ,)),
            dma((NZ,)),
            dma((NZ,)),
            dma((1,)),
        ],
        compiler_params=pltpu.CompilerParams(
            collective_id=0, has_side_effects=True, vmem_limit_bytes=48 * 2**20
        ),
    )(hidden_acts, out_grads, query_in, query_out, seq_ids)


def solution(mesh):
    placed = (P("dp", "mp"), P("dp", "mp"), P("dp", None, "mp"), P("dp", None, "mp"), P("dp", None))
    return jax.shard_map(body, mesh=mesh, in_specs=placed, out_specs=P("dp", "mp"), check_vma=False)
```

```python
import functools
import math

import jax
import jax.numpy as jnp
from jax import lax
from jax.experimental import pallas as pl
from jax.experimental.pallas import tpu as pltpu
from jax.sharding import PartitionSpec as P

R = 32
TOK = 640
SEQS = 16
NZ = 8
SIDE = 4
CHIPS = SIDE * SIDE
QH = 4
MESH = pl.DeviceIdType.MESH
NT = (((1,), (1,)), ((), ()))
TILES = TOK // 128
WIDE = TOK + 128
SCALE = 1.0 / math.sqrt(R * TOK / SEQS)


def kernel(
    hid, grad, q_in, q_out, seq, out,
    h_buf, g_buf, own_a, own_b, ring_a, ring_b, ids, proj, part, got, last, landed,
    loc_sem, sib_send, sib_recv, z_send, z_recv, a_send, a_recv, f_send, f_recv,
):
    z, m = lax.axis_index("dp"), lax.axis_index("mp")
    core = lax.rem(m, 2)
    chip = m // 2
    y, x = chip // SIDE, lax.rem(chip, SIDE)
    sibling = (z, chip * 2 + 1 - core)
    along = ((lax.rem(z + 1, NZ), m), (lax.rem(z + NZ - 1, NZ), m))

    mine = pl.ds(core * QH, QH)
    local = [
        pltpu.make_async_copy(src, dst, loc_sem.at[i])
        for i, (src, dst) in enumerate((
            (q_in.at[mine], own_a.at[0]),
            (q_out.at[mine], own_b.at[0]),
            (hid, h_buf.at[0]),
            (grad, g_buf.at[0]),
            (seq, ids),
        ))
    ]
    for copy in local:
        copy.start()

    ready = pltpu.get_barrier_semaphore()
    for target in along:
        pl.semaphore_signal(ready, inc=1, device_id=target, device_id_type=MESH)

    def greet(k, carry):
        pl.semaphore_signal(ready, inc=1, device_id=(z, lax.rem(m + k, 2 * CHIPS)), device_id_type=MESH)
        return carry

    lax.fori_loop(1, 2 * CHIPS, greet, 0)
    pl.semaphore_wait(ready, 2 * CHIPS + 1)

    def to_sibling(i, src, dst):
        return pltpu.make_async_remote_copy(src, dst, sib_send.at[i], sib_recv.at[i], sibling, MESH)

    theirs = pl.ds((1 - core) * QH, QH)
    swap = [
        to_sibling(0, q_in.at[theirs], own_a.at[1]),
        to_sibling(1, q_out.at[theirs], own_b.at[1]),
        to_sibling(2, hid, h_buf.at[1]),
        to_sibling(3, grad, g_buf.at[1]),
    ]

    def hop(d, s, j):
        if s > 0:
            a, b = ring_a.at[d, s - 1, j], ring_b.at[d, s - 1, j]
        elif j == 0:
            a, b = q_in.at[mine], q_out.at[mine]
        else:
            a, b = own_a.at[1], own_b.at[1]
        return [
            pltpu.make_async_remote_copy(
                src, dst.at[d, s, j], z_send.at[d, s, j, i], z_recv.at[d, s, j, i], along[d], MESH
            )
            for i, (src, dst) in enumerate(((a, ring_a), (b, ring_b)))
        ]

    hops = {(d, s, j): hop(d, s, j) for s in range(4) for j in range(2) for d in range(2) if s < 3 or d == j}

    def start(copies):
        for copy in copies:
            copy.start()

    def arrived(copies):
        for copy in copies:
            copy.wait_recv()

    start(swap[:2])
    for d in range(2):
        start(hops[d, 0, 0])
    start(swap[2:])
    arrived(swap[:2])
    for d in range(2):
        start(hops[d, 0, 1])

    def project(p, halves):
        for which, tokens in enumerate((h_buf, g_buf)):
            total = None
            for j, half in enumerate(halves):
                rows = half[which][...].reshape(QH * R, tokens.shape[2])
                term = lax.dot_general(rows, tokens[j], NT, preferred_element_type=jnp.float32)
                total = term if total is None else total + term
            proj[which] = total.reshape(CHIPS, 8, TOK)

        row = lax.broadcasted_iota(jnp.int32, (8, 128), 0)

        def pack(i, carry):
            for t in range(TILES):
                at = slice(t * 128, (t + 1) * 128)
                coded = []
                for which in range(2):
                    value = proj[which, i, :, at]
                    top = jnp.max(jnp.abs(value), axis=0, keepdims=True)
                    power = jnp.ceil(jnp.log2(jnp.maximum(top, 2.0**-100) * 1.0001)) - 15.0
                    coded.append(jnp.round(value * jnp.exp2(-power)))
                    carry = carry[:which] + (jnp.where(row == t, power, carry[which]),) + carry[which + 1 :]
                part[p, i, :, at] = jnp.concatenate(coded, axis=0).astype(jnp.int32).astype(jnp.int16)
            part[p, i, :, TOK:] = jnp.concatenate(carry, axis=0).astype(jnp.int32).astype(jnp.int16)
            return carry

        none = jnp.zeros((8, 128), jnp.float32)
        lax.fori_loop(0, CHIPS, pack, (none, none))

    def peer(k):
        return lax.rem(y + k // SIDE, SIDE) * SIDE + lax.rem(x + lax.rem(k, SIDE), SIDE)

    def spread(p):
        def send(k, carry):
            target = peer(k)
            pltpu.make_async_remote_copy(
                part.at[p, target], got.at[p, k - 1], a_send.at[p], a_recv.at[p], (z, target * 2 + core), MESH
            ).start()
            return carry

        lax.fori_loop(1, CHIPS, send, 0)

    label = lax.broadcasted_iota(jnp.int32, (SEQS, 128), 0)

    def add_up(p):
        pltpu.make_async_copy(got.at[p], got.at[p], a_recv.at[p]).wait()
        lanes = jnp.zeros((SEQS, 128), jnp.float32)
        powers = []
        for k in range(CHIPS):
            message = part.at[p, chip] if k == 0 else got.at[p, k - 1]
            powers.append(jnp.exp2(message[:, TOK:].astype(jnp.int32).astype(jnp.float32)))
        for t in range(TILES):
            at = slice(t * 128, (t + 1) * 128)
            total = [jnp.zeros((8, 128), jnp.float32)] * 2
            for k in range(CHIPS):
                message = part.at[p, chip] if k == 0 else got.at[p, k - 1]
                value = message[:, at].astype(jnp.int32).astype(jnp.float32)
                for which in range(2):
                    power = powers[k][which * 8 + t : which * 8 + t + 1]
                    total[which] = total[which] + value[which * 8 : which * 8 + 8] * power
            score = jnp.sum(total[0] * total[1], axis=0, keepdims=True)
            lanes = lanes + jnp.where(ids[:, at] == label, score, 0.0)
        last[p] = lanes

    def final_copy(p, step):
        origin = lax.rem(z + step + NZ, NZ)
        owner = (2 * origin + core) * 2 + chip // 8
        slot = lax.rem(chip, 8)
        away = pltpu.make_async_remote_copy(
            last.at[p], landed.at[slot], f_send.at[p], f_recv.at[0], (z, owner), MESH
        )
        here = pltpu.make_async_copy(last.at[p], landed.at[slot], f_recv.at[0])
        return owner == m, away, here

    steps = [0, -1, 1, -2, 2, -3, 3, 4]

    def finish(p):
        add_up(p)
        own, away, here = final_copy(p, steps[p])
        pl.when(own)(here.start)
        pl.when(jnp.logical_not(own))(away.start)

    for copy in local:
        copy.wait()
    arrived(swap[2:])
    project(0, [(own_a.at[0], own_b.at[0]), (own_a.at[1], own_b.at[1])])
    spread(0)
    for s in range(3):
        for j in range(2):
            for d in range(2):
                arrived(hops[d, s, j])
                if (d, s + 1, j) in hops:
                    start(hops[d, s + 1, j])
        for d in range(2):
            p = 1 + 2 * s + d
            project(p, [(ring_a.at[d, s, j], ring_b.at[d, s, j]) for j in range(2)])
            spread(p)
        for p in ([0] if s == 0 else [2 * s - 1, 2 * s]):
            finish(p)
    for d in range(2):
        arrived(hops[d, 3, d])
    project(7, [(ring_a.at[j, 3, j], ring_b.at[j, 3, j]) for j in range(2)])
    spread(7)
    for p in (5, 6, 7):
        finish(p)

    for copy in swap:
        copy.wait_send()
    for copies in hops.values():
        for copy in copies:
            copy.wait_send()
    for p in range(NZ):
        pltpu.make_async_copy(got.at[p], got.at[p], a_send.at[p]).wait()
        own, away, here = final_copy(p, steps[p])
        pl.when(jnp.logical_not(own))(away.wait_send)

    pltpu.make_async_copy(landed, landed, f_recv.at[0]).wait()
    for q in range(2):
        total = (landed[4 * q] + landed[4 * q + 1]) + (landed[4 * q + 2] + landed[4 * q + 3])
        out[:, q : q + 1] = jnp.sum(total, axis=1, keepdims=True) * SCALE


def body(hidden_acts, out_grads, query_in, query_out, seq_ids):
    ff, width = hidden_acts.shape[1], out_grads.shape[1]
    hbm_spec = pl.BlockSpec(memory_space=pltpu.MemorySpace.HBM)
    vmem_spec = pl.BlockSpec(memory_space=pltpu.VMEM)
    dma = pltpu.SemaphoreType.DMA
    bf16, f32 = jnp.bfloat16, jnp.float32
    return pl.pallas_call(
        kernel,
        out_shape=jax.ShapeDtypeStruct((SEQS, 2), f32),
        in_specs=[hbm_spec] * 5,
        out_specs=vmem_spec,
        scratch_shapes=[
            pltpu.VMEM((2, TOK, ff), bf16),
            pltpu.VMEM((2, TOK, width), bf16),
            pltpu.VMEM((2, QH, R, ff), bf16),
            pltpu.VMEM((2, QH, R, width), bf16),
            pltpu.VMEM((2, 4, 2, QH, R, ff), bf16),
            pltpu.VMEM((2, 4, 2, QH, R, width), bf16),
            pltpu.VMEM((1, TOK), jnp.int32),
            pltpu.VMEM((2, CHIPS, 8, TOK), f32),
            pltpu.VMEM((NZ, CHIPS, 16, WIDE), jnp.int16),
            pltpu.VMEM((NZ, CHIPS - 1, 16, WIDE), jnp.int16),
            pltpu.VMEM((NZ, SEQS, 128), f32),
            pltpu.VMEM((8, SEQS, 128), f32),
            dma((5,)),
            dma((4,)),
            dma((4,)),
            dma((2, 4, 2, 2)),
            dma((2, 4, 2, 2)),
            dma((NZ,)),
            dma((NZ,)),
            dma((NZ,)),
            dma((1,)),
        ],
        compiler_params=pltpu.CompilerParams(
            collective_id=0, has_side_effects=True, vmem_limit_bytes=63 * 2**20
        ),
    )(hidden_acts, out_grads, query_in, query_out, seq_ids)


def solution(mesh):
    placed = (P("dp", "mp"), P("dp", "mp"), P("dp", None, "mp"), P("dp", None, "mp"), P("dp", None))
    return jax.shard_map(body, mesh=mesh, in_specs=placed, out_specs=P("dp", "mp"), check_vma=False)
```

```python
import functools
import math

import jax
import jax.numpy as jnp
from jax import lax
from jax.experimental import pallas as pl
from jax.experimental.pallas import tpu as pltpu
from jax.sharding import PartitionSpec as P

R = 32
TOK = 640
SEQS = 16
NZ = 8
SIDE = 4
CHIPS = SIDE * SIDE
QH = 4
QC = 2
MESH = pl.DeviceIdType.MESH
NT = (((1,), (1,)), ((), ()))
TILES = TOK // 128
WIDE = TOK + 128
SCALE = 1.0 / math.sqrt(R * TOK / SEQS)


def kernel(
    hid, grad, q_in, q_out, seq, out,
    h_buf, g_buf, own, ring, ids, proj, part, got, last, landed,
    loc_sem, sib_send, sib_recv, z_send, z_recv, a_send, a_recv, f_send, f_recv, known,
):
    z, m = lax.axis_index("dp"), lax.axis_index("mp")
    core = lax.rem(m, 2)
    chip = m // 2
    y, x = chip // SIDE, lax.rem(chip, SIDE)

    def at(row, column):
        return (z, (lax.rem(row + SIDE, SIDE) * SIDE + lax.rem(column + SIDE, SIDE)) * 2 + core)

    sibling = (z, chip * 2 + 1 - core)
    along = ((lax.rem(z + 1, NZ), m), (lax.rem(z + NZ - 1, NZ), m))
    beside_x = (at(y, x + 1), at(y, x - 1))
    beside_y = (at(y + 1, x), at(y - 1, x))

    ff = hid.shape[1]

    def queries(of_core, half):
        return pl.ds(of_core * QH + half * QC, QC)

    local = [
        pltpu.make_async_copy(src, dst, loc_sem.at[i])
        for i, (src, dst) in enumerate((
            (q_in.at[queries(core, 0)], own.at[0, 0, :, :, :ff]),
            (q_out.at[queries(core, 0)], own.at[0, 0, :, :, ff:]),
            (q_in.at[queries(core, 1)], own.at[0, 1, :, :, :ff]),
            (q_out.at[queries(core, 1)], own.at[0, 1, :, :, ff:]),
            (hid, h_buf.at[0]),
            (grad, g_buf.at[0]),
            (seq, ids),
        ))
    ]
    for copy in local:
        copy.start()

    ready = pltpu.get_barrier_semaphore()
    for target in (*along, sibling, *beside_x, *beside_y):
        pl.semaphore_signal(ready, inc=1, device_id=target, device_id_type=MESH)
    pl.semaphore_wait(ready, 7)

    swap = [
        pltpu.make_async_remote_copy(src, dst, sib_send.at[i], sib_recv.at[i], sibling, MESH)
        for i, (src, dst) in enumerate((
            (q_in.at[queries(1 - core, 0)], own.at[1, 0, :, :, :ff]),
            (q_out.at[queries(1 - core, 0)], own.at[1, 0, :, :, ff:]),
            (q_in.at[queries(1 - core, 1)], own.at[1, 1, :, :, :ff]),
            (q_out.at[queries(1 - core, 1)], own.at[1, 1, :, :, ff:]),
            (hid, h_buf.at[1]),
            (grad, g_buf.at[1]),
        ))
    ]

    def hop(d, s, h, j):
        src = own.at[j, h] if s == 0 else ring.at[s - 1, h, j, d]
        dst = ring.at[s, h if s < 3 else 0, j, d]
        return pltpu.make_async_remote_copy(
            src, dst, z_send.at[s, h, j, d], z_recv.at[s, h, j, d], along[d], MESH
        )

    hops = {
        (d, s, h, j): hop(d, s, h, j)
        for s in range(4) for h in range(2) for j in range(2) for d in range(2) if s < 3 or d == h
    }

    for copy in swap[:2]:
        copy.start()
    for copy in local[:4]:
        copy.wait()
    for d in range(2):
        hops[d, 0, 0, 0].start()
    for copy in swap[2:]:
        copy.start()
    for h in range(2):
        if h == 1:
            for d in range(2):
                hops[d, 0, 1, 0].start()
        for copy in swap[2 * h : 2 * h + 2]:
            copy.wait_recv()
        for d in range(2):
            hops[d, 0, h, 1].start()

    for i, targets in enumerate((beside_x, beside_y, beside_y, (sibling,))):
        for target in targets:
            pl.semaphore_signal(known.at[i], inc=1, device_id=target, device_id_type=MESH)
        pl.semaphore_wait(known.at[i], len(targets))

    row = lax.broadcasted_iota(jnp.int32, (8, 128), 0)

    def project(p, feature_halves):
        for which, (tokens, columns) in enumerate(((h_buf, slice(0, ff)), (g_buf, slice(ff, None)))):
            total = None
            for j, half in enumerate(feature_halves):
                rows = half[:, :, :, columns].reshape(QH * R, tokens.shape[2])
                term = lax.dot_general(rows, tokens[j], NT, preferred_element_type=jnp.float32)
                total = term if total is None else total + term
            proj[which] = total.reshape(CHIPS, 8, TOK)

        def pack(i, carry):
            for t in range(TILES):
                at = slice(t * 128, (t + 1) * 128)
                coded = []
                for which in range(2):
                    value = proj[which, i, :, at]
                    top = jnp.max(jnp.abs(value), axis=0, keepdims=True)
                    power = jnp.ceil(jnp.log2(jnp.maximum(top, 2.0**-100) * 1.0001)) - 15.0
                    coded.append(jnp.round(value * jnp.exp2(-power)))
                    carry = carry[:which] + (jnp.where(row == t, power, carry[which]),) + carry[which + 1 :]
                part[p, i, :, at] = jnp.concatenate(coded, axis=0).astype(jnp.int32).astype(jnp.int16)
            part[p, i, :, TOK:] = jnp.concatenate(carry, axis=0).astype(jnp.int32).astype(jnp.int16)
            return carry

        none = jnp.zeros((8, 128), jnp.float32)
        lax.fori_loop(0, CHIPS, pack, (none, none))

    def spread(p):
        def send(k, carry):
            target = lax.rem(y + k // SIDE, SIDE) * SIDE + lax.rem(x + lax.rem(k, SIDE), SIDE)
            pltpu.make_async_remote_copy(
                part.at[p, target], got.at[p, k - 1], a_send.at[p], a_recv.at[p], (z, target * 2 + core), MESH
            ).start()
            return carry

        lax.fori_loop(1, CHIPS, send, 0)

    label = lax.broadcasted_iota(jnp.int32, (SEQS, 128), 0)

    def add_up(p):
        pltpu.make_async_copy(got.at[p], got.at[p], a_recv.at[p]).wait()
        lanes = jnp.zeros((SEQS, 128), jnp.float32)
        powers = []
        for k in range(CHIPS):
            message = part.at[p, chip] if k == 0 else got.at[p, k - 1]
            powers.append(jnp.exp2(message[:, TOK:].astype(jnp.int32).astype(jnp.float32)))
        for t in range(TILES):
            at = slice(t * 128, (t + 1) * 128)
            total = [jnp.zeros((8, 128), jnp.float32)] * 2
            for k in range(CHIPS):
                message = part.at[p, chip] if k == 0 else got.at[p, k - 1]
                value = message[:, at].astype(jnp.int32).astype(jnp.float32)
                for which in range(2):
                    power = powers[k][which * 8 + t : which * 8 + t + 1]
                    total[which] = total[which] + value[which * 8 : which * 8 + 8] * power
            score = jnp.sum(total[0] * total[1], axis=0, keepdims=True)
            lanes = lanes + jnp.where(ids[:, at] == label, score, 0.0)
        last[p] = lanes

    upper = chip // 8

    def final_copy(p):
        if p in (0, 7):
            origin, half = z + (0 if p == 0 else 4), upper
        else:
            s, half = divmod(p - 1, 2)
            origin = z + NZ + (2 * upper - 1) * (s + 1)
        owner = (2 * lax.rem(origin, NZ) + core) * 2 + half
        slot = lax.rem(chip, 8)
        away = pltpu.make_async_remote_copy(
            last.at[p], landed.at[slot], f_send.at[p], f_recv.at[0], (z, owner), MESH
        )
        here = pltpu.make_async_copy(last.at[p], landed.at[slot], f_recv.at[0])
        return owner == m, away, here

    def finish(p):
        add_up(p)
        mine, away, here = final_copy(p)
        pl.when(mine)(here.start)
        pl.when(jnp.logical_not(mine))(away.start)

    for copy in local[4:]:
        copy.wait()
    for copy in swap[4:]:
        copy.wait_recv()
    project(0, [own.at[j] for j in range(2)])
    spread(0)
    for s in range(4):
        for h in range(2 if s < 3 else 1):
            for j in range(2):
                for d in range(2):
                    stop = (d, s, h if s < 3 else d, j)
                    hops[stop].wait_recv()
                    onward = (d, s + 1, h, j)
                    if onward in hops:
                        hops[onward].start()
            p = 1 + 2 * s + h
            project(p, [ring.at[s, h, j] for j in range(2)])
            spread(p)
            finish(p - 1)
    finish(7)

    for copy in swap:
        copy.wait_send()
    for copy in hops.values():
        copy.wait_send()
    for p in range(NZ):
        pltpu.make_async_copy(got.at[p], got.at[p], a_send.at[p]).wait()
        mine, away, here = final_copy(p)
        pl.when(jnp.logical_not(mine))(away.wait_send)

    pltpu.make_async_copy(landed, landed, f_recv.at[0]).wait()
    for q in range(2):
        total = (landed[4 * q] + landed[4 * q + 1]) + (landed[4 * q + 2] + landed[4 * q + 3])
        out[:, q : q + 1] = jnp.sum(total, axis=1, keepdims=True) * SCALE


def body(hidden_acts, out_grads, query_in, query_out, seq_ids):
    ff, width = hidden_acts.shape[1], out_grads.shape[1]
    hbm_spec = pl.BlockSpec(memory_space=pltpu.MemorySpace.HBM)
    vmem_spec = pl.BlockSpec(memory_space=pltpu.VMEM)
    dma = pltpu.SemaphoreType.DMA
    bf16, f32 = jnp.bfloat16, jnp.float32
    return pl.pallas_call(
        kernel,
        out_shape=jax.ShapeDtypeStruct((SEQS, 2), f32),
        in_specs=[hbm_spec] * 5,
        out_specs=vmem_spec,
        scratch_shapes=[
            pltpu.VMEM((2, TOK, ff), bf16),
            pltpu.VMEM((2, TOK, width), bf16),
            pltpu.VMEM((2, 2, QC, R, ff + width), bf16),
            pltpu.VMEM((4, 2, 2, 2, QC, R, ff + width), bf16),
            pltpu.VMEM((1, TOK), jnp.int32),
            pltpu.VMEM((2, CHIPS, 8, TOK), f32),
            pltpu.VMEM((NZ, CHIPS, 16, WIDE), jnp.int16),
            pltpu.VMEM((NZ, CHIPS - 1, 16, WIDE), jnp.int16),
            pltpu.VMEM((NZ, SEQS, 128), f32),
            pltpu.VMEM((8, SEQS, 128), f32),
            dma((7,)),
            dma((6,)),
            dma((6,)),
            dma((4, 2, 2, 2)),
            dma((4, 2, 2, 2)),
            dma((NZ,)),
            dma((NZ,)),
            dma((NZ,)),
            dma((1,)),
            pltpu.SemaphoreType.REGULAR((4,)),
        ],
        compiler_params=pltpu.CompilerParams(
            collective_id=0, has_side_effects=True, vmem_limit_bytes=63 * 2**20
        ),
    )(hidden_acts, out_grads, query_in, query_out, seq_ids)


def solution(mesh):
    placed = (P("dp", "mp"), P("dp", "mp"), P("dp", None, "mp"), P("dp", None, "mp"), P("dp", None))
    return jax.shard_map(body, mesh=mesh, in_specs=placed, out_specs=P("dp", "mp"), check_vma=False)
```

```python
import functools
import math

import jax
import jax.numpy as jnp
from jax import lax
from jax.experimental import pallas as pl
from jax.experimental.pallas import tpu as pltpu
from jax.sharding import PartitionSpec as P

R = 32
TOK = 640
SEQS = 16
NZ = 8
SIDE = 4
CHIPS = SIDE * SIDE
QH = 4
QC = 2
MESH = pl.DeviceIdType.MESH
NT = (((1,), (1,)), ((), ()))
TILES = TOK // 128
WIDE = TOK + 128
SCALE = 1.0 / math.sqrt(R * TOK / SEQS)


def kernel(
    hid, grad, q_in, q_out, seq, out,
    h_buf, g_buf, own, ring, ids, proj, part, got, last, landed,
    loc_sem, sib_send, sib_recv, z_send, z_recv, a_send, a_recv, f_send, f_recv, known,
):
    z, m = lax.axis_index("dp"), lax.axis_index("mp")
    core = lax.rem(m, 2)
    chip = m // 2
    y, x = chip // SIDE, lax.rem(chip, SIDE)

    def at(row, column):
        return (z, (lax.rem(row + SIDE, SIDE) * SIDE + lax.rem(column + SIDE, SIDE)) * 2 + core)

    sibling = (z, chip * 2 + 1 - core)
    along = ((lax.rem(z + 1, NZ), m), (lax.rem(z + NZ - 1, NZ), m))
    beside_x = (at(y, x + 1), at(y, x - 1))
    beside_y = (at(y + 1, x), at(y - 1, x))

    ff = hid.shape[1]

    def queries(of_core, half):
        return pl.ds(of_core * QH + half * QC, QC)

    local = [
        pltpu.make_async_copy(src, dst, loc_sem.at[i])
        for i, (src, dst) in enumerate((
            (q_in.at[queries(core, 0)], own.at[0, 0, :, :, :ff]),
            (q_out.at[queries(core, 0)], own.at[0, 0, :, :, ff:]),
            (q_in.at[queries(core, 1)], own.at[0, 1, :, :, :ff]),
            (q_out.at[queries(core, 1)], own.at[0, 1, :, :, ff:]),
            (hid, h_buf.at[0]),
            (grad, g_buf.at[0]),
            (seq, ids),
        ))
    ]
    for copy in local:
        copy.start()

    ready = pltpu.get_barrier_semaphore()
    for target in (*along, sibling, *beside_x, *beside_y):
        pl.semaphore_signal(ready, inc=1, device_id=target, device_id_type=MESH)
    pl.semaphore_wait(ready, 7)

    swap = [
        pltpu.make_async_remote_copy(src, dst, sib_send.at[i], sib_recv.at[i], sibling, MESH)
        for i, (src, dst) in enumerate((
            (q_in.at[queries(1 - core, 0)], own.at[1, 0, :, :, :ff]),
            (q_out.at[queries(1 - core, 0)], own.at[1, 0, :, :, ff:]),
            (q_in.at[queries(1 - core, 1)], own.at[1, 1, :, :, :ff]),
            (q_out.at[queries(1 - core, 1)], own.at[1, 1, :, :, ff:]),
            (hid, h_buf.at[1]),
            (grad, g_buf.at[1]),
        ))
    ]

    def hop(d, s, h, j):
        src = own.at[j, h] if s == 0 else ring.at[s - 1, h, j, d]
        dst = ring.at[s, h if s < 3 else 0, j, d]
        return pltpu.make_async_remote_copy(
            src, dst, z_send.at[s, h, j, d], z_recv.at[s, h, j, d], along[d], MESH
        )

    hops = {
        (d, s, h, j): hop(d, s, h, j)
        for s in range(4) for h in range(2) for j in range(2) for d in range(2) if s < 3 or d == h
    }

    for copy in swap[:2]:
        copy.start()
    for copy in local[:4]:
        copy.wait()
    for d in range(2):
        hops[d, 0, 0, 0].start()
    for copy in swap[2:]:
        copy.start()
    for h in range(2):
        if h == 1:
            for d in range(2):
                hops[d, 0, 1, 0].start()
        for copy in swap[2 * h : 2 * h + 2]:
            copy.wait_recv()
        for d in range(2):
            hops[d, 0, h, 1].start()

    for i, targets in enumerate((beside_x, beside_y, beside_y, (sibling,))):
        for target in targets:
            pl.semaphore_signal(known.at[i], inc=1, device_id=target, device_id_type=MESH)
        pl.semaphore_wait(known.at[i], len(targets))

    row = lax.broadcasted_iota(jnp.int32, (8, 128), 0)

    steps_away = sorted(range(1, CHIPS), key=lambda k: -sum(min(i, SIDE - i) for i in divmod(k, SIDE)))

    def project(p, feature_halves):
        for j, half in enumerate(feature_halves):
            half = half()
            for which, (tokens, columns) in enumerate(((h_buf, slice(0, ff)), (g_buf, slice(ff, None)))):
                rows = half[:, :, :, columns].reshape(QH * R, tokens.shape[2])
                term = lax.dot_general(rows, tokens[j], NT, preferred_element_type=jnp.float32)
                term = term.reshape(CHIPS, 8, TOK)
                if j == 0:
                    proj[which] = term
                else:
                    proj[which] += term

        def pack(i):
            powers = [jnp.zeros((8, 128), jnp.float32)] * 2
            for t in range(TILES):
                at = slice(t * 128, (t + 1) * 128)
                coded = []
                for which in range(2):
                    value = proj[which, i, :, at]
                    top = jnp.max(jnp.abs(value), axis=0, keepdims=True)
                    power = jnp.ceil(jnp.log2(jnp.maximum(top, 2.0**-100) * 1.0001)) - 15.0
                    coded.append(jnp.round(value * jnp.exp2(-power)))
                    powers[which] = jnp.where(row == t, power, powers[which])
                part[p, i, :, at] = jnp.concatenate(coded, axis=0).astype(jnp.int32).astype(jnp.int16)
            part[p, i, :, TOK:] = jnp.concatenate(powers, axis=0).astype(jnp.int32).astype(jnp.int16)

        for k in steps_away:
            target = lax.rem(y + k // SIDE, SIDE) * SIDE + lax.rem(x + k % SIDE, SIDE)
            pack(target)
            pltpu.make_async_remote_copy(
                part.at[p, target], got.at[p, k - 1], a_send.at[p], a_recv.at[p], (z, target * 2 + core), MESH
            ).start()
        pack(chip)

    label = lax.broadcasted_iota(jnp.int32, (SEQS, 128), 0)

    def add_up(p):
        pltpu.make_async_copy(got.at[p], got.at[p], a_recv.at[p]).wait()
        lanes = jnp.zeros((SEQS, 128), jnp.float32)
        powers = []
        for k in range(CHIPS):
            message = part.at[p, chip] if k == 0 else got.at[p, k - 1]
            powers.append(jnp.exp2(message[:, TOK:].astype(jnp.int32).astype(jnp.float32)))
        for t in range(TILES):
            at = slice(t * 128, (t + 1) * 128)
            total = [jnp.zeros((8, 128), jnp.float32)] * 2
            for k in range(CHIPS):
                message = part.at[p, chip] if k == 0 else got.at[p, k - 1]
                value = message[:, at].astype(jnp.int32).astype(jnp.float32)
                for which in range(2):
                    power = powers[k][which * 8 + t : which * 8 + t + 1]
                    total[which] = total[which] + value[which * 8 : which * 8 + 8] * power
            score = jnp.sum(total[0] * total[1], axis=0, keepdims=True)
            lanes = lanes + jnp.where(ids[:, at] == label, score, 0.0)
        last[p] = lanes

    upper = chip // 8

    def final_copy(p):
        if p in (0, 7):
            origin, half = z + (0 if p == 0 else 4), upper
        else:
            s, half = divmod(p - 1, 2)
            origin = z + NZ + (2 * upper - 1) * (s + 1)
        owner = (2 * lax.rem(origin, NZ) + core) * 2 + half
        slot = lax.rem(chip, 8)
        away = pltpu.make_async_remote_copy(
            last.at[p], landed.at[slot], f_send.at[p], f_recv.at[0], (z, owner), MESH
        )
        here = pltpu.make_async_copy(last.at[p], landed.at[slot], f_recv.at[0])
        return owner == m, away, here

    def finish(p):
        add_up(p)
        mine, away, here = final_copy(p)
        pl.when(mine)(here.start)
        pl.when(jnp.logical_not(mine))(away.start)

    for copy in local[4:]:
        copy.wait()
    for copy in swap[4:]:
        copy.wait_recv()
    project(0, [functools.partial(lambda j: own.at[j], j) for j in range(2)])
    def arrival(s, h, j):
        for d in range(2):
            hops[d, s, h if s < 3 else d, j].wait_recv()
            if (d, s + 1, h, j) in hops:
                hops[d, s + 1, h, j].start()
        return ring.at[s, h, j]

    for s in range(4):
        for h in range(2 if s < 3 else 1):
            p = 1 + 2 * s + h
            project(p, [functools.partial(arrival, s, h, j) for j in range(2)])
            finish(p - 1)
    finish(7)

    for copy in swap:
        copy.wait_send()
    for copy in hops.values():
        copy.wait_send()
    for p in range(NZ):
        pltpu.make_async_copy(got.at[p], got.at[p], a_send.at[p]).wait()
        mine, away, here = final_copy(p)
        pl.when(jnp.logical_not(mine))(away.wait_send)

    pltpu.make_async_copy(landed, landed, f_recv.at[0]).wait()
    for q in range(2):
        total = (landed[4 * q] + landed[4 * q + 1]) + (landed[4 * q + 2] + landed[4 * q + 3])
        out[:, q : q + 1] = jnp.sum(total, axis=1, keepdims=True) * SCALE


def body(hidden_acts, out_grads, query_in, query_out, seq_ids):
    ff, width = hidden_acts.shape[1], out_grads.shape[1]
    hbm_spec = pl.BlockSpec(memory_space=pltpu.MemorySpace.HBM)
    vmem_spec = pl.BlockSpec(memory_space=pltpu.VMEM)
    dma = pltpu.SemaphoreType.DMA
    bf16, f32 = jnp.bfloat16, jnp.float32
    return pl.pallas_call(
        kernel,
        out_shape=pltpu.VMEM((SEQS, 2), f32),
        in_specs=[hbm_spec] * 5,
        out_specs=vmem_spec,
        scratch_shapes=[
            pltpu.VMEM((2, TOK, ff), bf16),
            pltpu.VMEM((2, TOK, width), bf16),
            pltpu.VMEM((2, 2, QC, R, ff + width), bf16),
            pltpu.VMEM((4, 2, 2, 2, QC, R, ff + width), bf16),
            pltpu.VMEM((1, TOK), jnp.int32),
            pltpu.VMEM((2, CHIPS, 8, TOK), f32),
            pltpu.VMEM((NZ, CHIPS, 16, WIDE), jnp.int16),
            pltpu.VMEM((NZ, CHIPS - 1, 16, WIDE), jnp.int16),
            pltpu.VMEM((NZ, SEQS, 128), f32),
            pltpu.VMEM((8, SEQS, 128), f32),
            dma((7,)),
            dma((6,)),
            dma((6,)),
            dma((4, 2, 2, 2)),
            dma((4, 2, 2, 2)),
            dma((NZ,)),
            dma((NZ,)),
            dma((NZ,)),
            dma((1,)),
            pltpu.SemaphoreType.REGULAR((4,)),
        ],
        compiler_params=pltpu.CompilerParams(
            collective_id=0, has_side_effects=True, vmem_limit_bytes=63 * 2**20
        ),
    )(hidden_acts, out_grads, query_in, query_out, seq_ids)


def solution(mesh):
    placed = (P("dp", "mp"), P("dp", "mp"), P("dp", None, "mp"), P("dp", None, "mp"), P("dp", None))
    return jax.shard_map(body, mesh=mesh, in_specs=placed, out_specs=P("dp", "mp"), check_vma=False)
```

```python
import functools
import math

import jax
import jax.numpy as jnp
from jax import lax
from jax.experimental import pallas as pl
from jax.experimental.pallas import tpu as pltpu
from jax.sharding import PartitionSpec as P

R = 32
TOK = 640
SEQS = 16
NZ = 8
SIDE = 4
CHIPS = SIDE * SIDE
QH = 4
QC = 2
MESH = pl.DeviceIdType.MESH
NT = (((1,), (1,)), ((), ()))
TILES = TOK // 128
WIDE = TOK + 128
SCALE = 1.0 / math.sqrt(R * TOK / SEQS)


def kernel(
    hid, grad, q_in, q_out, seq, out,
    h_buf, g_buf, own, ring, ids, proj, part, got, last, landed,
    loc_sem, sib_send, sib_recv, z_send, z_recv, a_send, a_recv, f_send, f_recv, x_send, known,
):
    z, m = lax.axis_index("dp"), lax.axis_index("mp")
    core = lax.rem(m, 2)
    chip = m // 2
    y, x = chip // SIDE, lax.rem(chip, SIDE)

    def at(row, column):
        return (z, (lax.rem(row + SIDE, SIDE) * SIDE + lax.rem(column + SIDE, SIDE)) * 2 + core)

    sibling = (z, chip * 2 + 1 - core)
    along = ((lax.rem(z + 1, NZ), m), (lax.rem(z + NZ - 1, NZ), m))
    beside = (at(y + core, x + 1 - core), at(y - core, x - 1 + core))

    ff = hid.shape[1]

    def queries(of_core, half):
        return pl.ds(of_core * QH + half * QC, QC)

    local = [
        pltpu.make_async_copy(src, dst, loc_sem.at[i])
        for i, (src, dst) in enumerate((
            (q_in.at[queries(core, 0)], own.at[0, 0, :, :, :ff]),
            (q_out.at[queries(core, 0)], own.at[0, 0, :, :, ff:]),
            (q_in.at[queries(core, 1)], own.at[0, 1, :, :, :ff]),
            (q_out.at[queries(core, 1)], own.at[0, 1, :, :, ff:]),
            (hid, h_buf.at[0]),
            (grad, g_buf.at[0]),
            (seq, ids),
        ))
    ]
    for copy in local:
        copy.start()

    ready = pltpu.get_barrier_semaphore()
    for target in (*along, sibling, *beside):
        pl.semaphore_signal(ready, inc=1, device_id=target, device_id_type=MESH)
    pl.semaphore_wait(ready, 5)

    swap = [
        pltpu.make_async_remote_copy(src, dst, sib_send.at[i], sib_recv.at[i], sibling, MESH)
        for i, (src, dst) in enumerate((
            (q_in.at[queries(1 - core, 0)], own.at[1, 0, :, :, :ff]),
            (q_out.at[queries(1 - core, 0)], own.at[1, 0, :, :, ff:]),
            (q_in.at[queries(1 - core, 1)], own.at[1, 1, :, :, :ff]),
            (q_out.at[queries(1 - core, 1)], own.at[1, 1, :, :, ff:]),
            (hid, h_buf.at[1]),
            (grad, g_buf.at[1]),
        ))
    ]

    def hop(d, s, h, j):
        src = own.at[j, h] if s == 0 else ring.at[s - 1, h, j, d]
        dst = ring.at[s, h if s < 3 else 0, j, d]
        return pltpu.make_async_remote_copy(
            src, dst, z_send.at[s, h, j, d], z_recv.at[s, h, j, d], along[d], MESH
        )

    def late_part(query):
        return ring.at[3, 0, 1, 0, query]

    short = pltpu.make_async_remote_copy(
        ring.at[2, 0, 1, 0, 0], late_part(0), z_send.at[3, 0, 1, 0], z_recv.at[3, 0, 1, 0], along[0], MESH
    )
    extra = pltpu.make_async_remote_copy(
        ring.at[2, 0, 1, 1, 1], late_part(1), x_send.at[0], z_recv.at[3, 0, 1, 0], along[1], MESH
    )

    hops = {
        (d, s, h, j): hop(d, s, h, j)
        for s in range(4) for h in range(2) for j in range(2) for d in range(2) if s < 3 or d == h
    }

    for copy in swap[:2]:
        copy.start()
    for copy in local[:4]:
        copy.wait()
    for d in range(2):
        hops[d, 0, 0, 0].start()
    for copy in swap[2:]:
        copy.start()
    for h in range(2):
        if h == 1:
            for d in range(2):
                hops[d, 0, 1, 0].start()
        for copy in swap[2 * h : 2 * h + 2]:
            copy.wait_recv()
        for d in range(2):
            hops[d, 0, h, 1].start()

    for i, targets in enumerate((beside, beside, (sibling,), beside, beside)):
        for target in targets:
            pl.semaphore_signal(known.at[i], inc=1, device_id=target, device_id_type=MESH)
        pl.semaphore_wait(known.at[i], len(targets))

    row = lax.broadcasted_iota(jnp.int32, (8, 128), 0)

    steps_away = sorted(range(1, CHIPS), key=lambda k: -sum(min(i, SIDE - i) for i in divmod(k, SIDE)))

    def project(p, feature_halves):
        for j, half in enumerate(feature_halves):
            half = half()
            for which, (tokens, columns) in enumerate(((h_buf, slice(0, ff)), (g_buf, slice(ff, None)))):
                rows = half[:, :, :, columns].reshape(QH * R, tokens.shape[2])
                term = lax.dot_general(rows, tokens[j], NT, preferred_element_type=jnp.float32)
                term = term.reshape(CHIPS, 8, TOK)
                if j == 0:
                    proj[which] = term
                else:
                    proj[which] += term

        def pack(i):
            powers = [jnp.zeros((8, 128), jnp.float32)] * 2
            for t in range(TILES):
                at = slice(t * 128, (t + 1) * 128)
                coded = []
                for which in range(2):
                    value = proj[which, i, :, at]
                    top = jnp.max(jnp.abs(value), axis=0, keepdims=True)
                    power = jnp.ceil(jnp.log2(jnp.maximum(top, 2.0**-100) * 1.0001)) - 15.0
                    coded.append(jnp.round(value * jnp.exp2(-power)))
                    powers[which] = jnp.where(row == t, power, powers[which])
                part[p, i, :, at] = jnp.concatenate(coded, axis=0).astype(jnp.int32).astype(jnp.int16)
            part[p, i, :, TOK:] = jnp.concatenate(powers, axis=0).astype(jnp.int32).astype(jnp.int16)

        for k in steps_away:
            target = lax.rem(y + k // SIDE, SIDE) * SIDE + lax.rem(x + k % SIDE, SIDE)
            pack(target)
            pltpu.make_async_remote_copy(
                part.at[p, target], got.at[p, k - 1], a_send.at[p], a_recv.at[p], (z, target * 2 + core), MESH
            ).start()
        pack(chip)

    label = lax.broadcasted_iota(jnp.int32, (SEQS, 128), 0)

    def add_up(p):
        pltpu.make_async_copy(got.at[p], got.at[p], a_recv.at[p]).wait()
        lanes = jnp.zeros((SEQS, 128), jnp.float32)
        powers = []
        for k in range(CHIPS):
            message = part.at[p, chip] if k == 0 else got.at[p, k - 1]
            powers.append(jnp.exp2(message[:, TOK:].astype(jnp.int32).astype(jnp.float32)))
        for t in range(TILES):
            at = slice(t * 128, (t + 1) * 128)
            total = [jnp.zeros((8, 128), jnp.float32)] * 2
            for k in range(CHIPS):
                message = part.at[p, chip] if k == 0 else got.at[p, k - 1]
                value = message[:, at].astype(jnp.int32).astype(jnp.float32)
                for which in range(2):
                    power = powers[k][which * 8 + t : which * 8 + t + 1]
                    total[which] = total[which] + value[which * 8 : which * 8 + 8] * power
            score = jnp.sum(total[0] * total[1], axis=0, keepdims=True)
            lanes = lanes + jnp.where(ids[:, at] == label, score, 0.0)
        last[p] = lanes

    upper = chip // 8

    def final_copy(p):
        if p in (0, 7):
            origin, half = z + (0 if p == 0 else 4), upper
        else:
            s, half = divmod(p - 1, 2)
            origin = z + NZ + (2 * upper - 1) * (s + 1)
        owner = (2 * lax.rem(origin, NZ) + core) * 2 + half
        slot = lax.rem(chip, 8)
        away = pltpu.make_async_remote_copy(
            last.at[p], landed.at[slot], f_send.at[p], f_recv.at[0], (z, owner), MESH
        )
        here = pltpu.make_async_copy(last.at[p], landed.at[slot], f_recv.at[0])
        return owner == m, away, here

    def finish(p):
        add_up(p)
        mine, away, here = final_copy(p)
        pl.when(mine)(here.start)
        pl.when(jnp.logical_not(mine))(away.start)

    for copy in local[4:]:
        copy.wait()
    for copy in swap[4:]:
        copy.wait_recv()
    project(0, [functools.partial(lambda j: own.at[j], j) for j in range(2)])
    def arrival(s, h, j):
        for d in range(2):
            hops[d, s, h if s < 3 else d, j].wait_recv()
            onward = (d, s + 1, h, j)
            if onward == (0, 3, 0, 1):
                pl.when(z == NZ - 1)(short.start)
                pl.when(z != NZ - 1)(hops[onward].start)
            elif onward in hops:
                hops[onward].start()
            if (d, s, h, j) == (1, 2, 0, 1):
                pl.when(z == 1)(extra.start)
        return ring.at[s, h, j]

    for s in range(4):
        for h in range(2 if s < 3 else 1):
            p = 1 + 2 * s + h
            project(p, [functools.partial(arrival, s, h, j) for j in range(2)])
            finish(p - 1)
    finish(7)

    for copy in swap:
        copy.wait_send()
    for onward, copy in hops.items():
        if onward == (0, 3, 0, 1):
            pl.when(z == NZ - 1)(short.wait_send)
            pl.when(z != NZ - 1)(copy.wait_send)
        else:
            copy.wait_send()
    pl.when(z == 1)(extra.wait_send)
    for p in range(NZ):
        pltpu.make_async_copy(got.at[p], got.at[p], a_send.at[p]).wait()
        mine, away, here = final_copy(p)
        pl.when(jnp.logical_not(mine))(away.wait_send)

    pltpu.make_async_copy(landed, landed, f_recv.at[0]).wait()
    for q in range(2):
        total = (landed[4 * q] + landed[4 * q + 1]) + (landed[4 * q + 2] + landed[4 * q + 3])
        out[:, q : q + 1] = jnp.sum(total, axis=1, keepdims=True) * SCALE


def body(hidden_acts, out_grads, query_in, query_out, seq_ids):
    ff, width = hidden_acts.shape[1], out_grads.shape[1]
    hbm_spec = pl.BlockSpec(memory_space=pltpu.MemorySpace.HBM)
    vmem_spec = pl.BlockSpec(memory_space=pltpu.VMEM)
    dma = pltpu.SemaphoreType.DMA
    bf16, f32 = jnp.bfloat16, jnp.float32
    return pl.pallas_call(
        kernel,
        out_shape=pltpu.VMEM((SEQS, 2), f32),
        in_specs=[hbm_spec] * 5,
        out_specs=vmem_spec,
        scratch_shapes=[
            pltpu.VMEM((2, TOK, ff), bf16),
            pltpu.VMEM((2, TOK, width), bf16),
            pltpu.VMEM((2, 2, QC, R, ff + width), bf16),
            pltpu.VMEM((4, 2, 2, 2, QC, R, ff + width), bf16),
            pltpu.VMEM((1, TOK), jnp.int32),
            pltpu.VMEM((2, CHIPS, 8, TOK), f32),
            pltpu.VMEM((NZ, CHIPS, 16, WIDE), jnp.int16),
            pltpu.VMEM((NZ, CHIPS - 1, 16, WIDE), jnp.int16),
            pltpu.VMEM((NZ, SEQS, 128), f32),
            pltpu.VMEM((8, SEQS, 128), f32),
            dma((7,)),
            dma((6,)),
            dma((6,)),
            dma((4, 2, 2, 2)),
            dma((4, 2, 2, 2)),
            dma((NZ,)),
            dma((NZ,)),
            dma((NZ,)),
            dma((1,)),
            dma((1,)),
            pltpu.SemaphoreType.REGULAR((5,)),
        ],
        compiler_params=pltpu.CompilerParams(
            collective_id=0, has_side_effects=True, vmem_limit_bytes=63 * 2**20
        ),
    )(hidden_acts, out_grads, query_in, query_out, seq_ids)


def solution(mesh):
    placed = (P("dp", "mp"), P("dp", "mp"), P("dp", None, "mp"), P("dp", None, "mp"), P("dp", None))
    return jax.shard_map(body, mesh=mesh, in_specs=placed, out_specs=P("dp", "mp"), check_vma=False)
```
